32 devices in a mesh: groups: 2 (over y), rows: 4 (over x, core), heads: 4 (over z).
Axes of the slice: x: 2, y: 2, z: 4, core: 2. Of those that a mesh axis runs over, the one named last changes fastest.
Arguments:
- hidden: bfloat16 [32, 4096], P(('groups', 'rows')), parts along dimension 0, may hold values from -6 to 6
- parent: int32 [32], P('groups'), parts along dimension 0, may hold values from 0 to 7
- ssm_state: bfloat16 [32, 64, 64, 256], P(('groups', 'rows'), 'heads'), parts along dimension 0, may hold values from -10 to 10, as said below
- conv_x: bfloat16 [32, 3, 4096], P(('groups', 'rows'), None, 'heads'), parts along dimension 0, may hold values from -6 to 6
- conv_bc: bfloat16 [32, 3, 512], P(('groups', 'rows'), None, 'heads'), parts along dimension 0, may hold values from -6 to 6
- w_gate: bfloat16 [4096, 4096], P(None, 'heads'), may hold values from -0.09375 to 0.09375
- w_x: bfloat16 [4096, 4096], P(None, 'heads'), may hold values from -0.09375 to 0.09375
- w_bc: bfloat16 [4096, 512], P(None, 'heads'), may hold values from -0.09375 to 0.09375
- w_dt: bfloat16 [4096, 64], P(None, 'heads'), may hold values from -0.09375 to 0.09375
- dt_bias: float32 [64], P('heads'), may hold values from -1 to 1
- a_log: float32 [64], P('heads'), may hold values from -1.5 to 1
- d_skip: float32 [64], P('heads'), may hold values from 0.5 to 2
- conv_wx: bfloat16 [4, 4096], P(None, 'heads'), may hold values from -3 to 3
- conv_wbc: bfloat16 [4, 512], P(None, 'heads'), may hold values from -3 to 3
- norm_gain: float32 [4096], P('heads'), may hold values from 0.1 to 1.9
- w_out: bfloat16 [4096, 4096], P('heads'), may hold values from -0.09375 to 0.09375
Outputs:
- mixed: bfloat16 [32, 4096], P(('groups', 'rows'), 'heads'), parts along dimension 0
- new_state: bfloat16 [32, 64, 64, 256], P(('groups', 'rows'), 'heads'), parts along dimension 0
- new_conv_x: bfloat16 [32, 3, 4096], P(('groups', 'rows'), None, 'heads'), parts along dimension 0
- new_conv_bc: bfloat16 [32, 3, 512], P(('groups', 'rows'), None, 'heads'), parts along dimension 0
The draws below stay inside these ranges and needn't reach their ends.
There are 2 independent parts, one for each index of `groups`. The reference program is written for one: setup_inputs(seed, part) draws one part's arguments, and reference() takes and returns one part's arrays. A program takes and returns all parts, laid end to end along the dimension named above; an argument that names none is the same for every part. Nothing has to cross between parts.
Inputs may be any that keep to these rules, and one draw needn't show every extreme that they name: `ssm_state`: recurrent state of each row and head.
All inputs are finite; a program needn't handle non-finite values.
Results may differ from the reference program's by a relative error of at most 0.0095.
Values may be sent and summed in bfloat16 or wider, within the bound.
A program may use at most 128 MiB of HBM per device.

```python
import math
import jax
import jax.numpy as jnp
import numpy as np
from jax import lax

D = 4096
HEADS = 64
HEAD_DIM = 64
STATE = 256
KCONV = 4
BEAMS = 8
ROWS = 16
INNER = 4096
BCW = 512


def draw_ssm_state(key, part):
    key = jax.random.fold_in(key, 7)
    level = jnp.arange(HEADS, dtype=jnp.float32) / (HEADS - 1)
    head_scale = (0.5 * 3.0 ** level).reshape(1, HEADS, 1, 1)
    shape = (ROWS, HEADS, HEAD_DIM, STATE)
    base = jnp.clip(jax.random.normal(key, shape, jnp.float32), -4.0, 4.0)
    return (base * head_scale).astype(jnp.bfloat16)


def touch_ends(array, rng, least, top_value):
    extent = array.shape
    spot = [jax.random.randint(jax.random.fold_in(rng, axis), (), 0, extent[axis]) for axis in range(len(extent))]
    array = array.at[tuple(spot)].set(least)
    longest = extent.index(max(extent))
    spot[longest] = (spot[longest] + 1) % extent[longest]
    return array.at[tuple(spot)].set(top_value)


def block_levels(key, extent, pieces, low, largest):
    level = 1.0
    for position, shards_of in pieces:
        steps = jax.random.uniform(jax.random.fold_in(jax.random.fold_in(key, 6), position), (shards_of,), jnp.float32, low / len(pieces), largest / len(pieces))
        level = level * jnp.repeat(jnp.exp(steps), extent[position] // shards_of).reshape((-1,) + (1,) * (len(extent) - 1 - position))
    return level


def rank_table(number_of, skew):
    portions = [(1 << 20) // math.isqrt(grade ** skew) + 1 for grade in range(1, number_of + 1)]
    width = 1 + sum(portions) // (1 << 30)
    return np.cumsum(np.array([max(1, weight // width) for weight in portions]))


def skewed_ids(stream_key, shape, number_of, lean):
    listing = rank_table(number_of, lean)
    ticket = jax.random.randint(jax.random.fold_in(stream_key, 1), shape, 0, int(listing[number_of - 1]))
    rank = jnp.searchsorted(jnp.asarray(listing, jnp.int32), ticket, side="right")
    return jax.random.permutation(jax.random.fold_in(stream_key, 2), number_of)[rank].astype(jnp.int32)


def bell_draw(rng, shape, deviation, most, pieces=(), held_as=jnp.bfloat16):
    entries = jax.random.normal(rng, shape, jnp.float32) * deviation
    if len(pieces) > 0:
        entries = block_levels(rng, shape, pieces, -0.22, 0.18) * entries
    return jnp.clip(entries, min=-most, max=most).astype(held_as)


def setup_inputs(seed: int = 0, part: int = 0) -> dict:
    key_of = jax.random.split(jax.random.key(seed), 17)
    own_keys = jax.random.split(jax.random.fold_in(key_of[16], part), 17)
    hidden = bell_draw(own_keys[0], (ROWS, D), 1.0, 6.0, ((0, 4),))
    parent = touch_ends(skewed_ids(own_keys[1], (ROWS,), BEAMS, 2), jax.random.fold_in(own_keys[1], 3), 0, BEAMS - 1).astype(jnp.int32)
    ssm_state = draw_ssm_state(jax.random.fold_in(jax.random.fold_in(key_of[16], part), 71), part)
    conv_x = bell_draw(own_keys[3], (ROWS, KCONV - 1, INNER), 1.0, 6.0, ((0, 4), (2, 4)))
    conv_bc = bell_draw(own_keys[4], (ROWS, KCONV - 1, BCW), 1.0, 6.0, ((0, 4), (2, 4)))
    w_gate = bell_draw(key_of[5], (D, INNER), D ** -0.5, 0.09375, ((1, 4),))
    w_x = bell_draw(key_of[6], (D, INNER), D ** -0.5, 0.09375, ((1, 4),))
    w_bc = bell_draw(key_of[7], (D, BCW), D ** -0.5, 0.09375, ((1, 4),))
    w_dt = bell_draw(key_of[8], (D, HEADS), D ** -0.5, 0.09375, ((1, 4),))
    dt_bias = jnp.clip(jax.random.uniform(key_of[9], (HEADS,), jnp.float32, -1.0, 1.0) * block_levels(key_of[9], (HEADS,), ((0, 4),), -0.4, 0.0), -1.0, 1.0)
    a_log = jnp.clip(-1.5 + 2.5 * jax.random.uniform(key_of[10], (HEADS,), jnp.float32) ** block_levels(key_of[10], (HEADS,), ((0, 4),), -0.2, 0.2), -1.5, 1.0)
    d_skip = jnp.clip(0.5 + 1.5 * jax.random.uniform(key_of[11], (HEADS,), jnp.float32) ** block_levels(key_of[11], (HEADS,), ((0, 4),), -0.2, 0.2), 0.5, 2.0)
    conv_wx = bell_draw(key_of[12], (KCONV, INNER), KCONV ** -0.5, 3.0, ((1, 4),))
    conv_wbc = bell_draw(key_of[13], (KCONV, BCW), KCONV ** -0.5, 3.0, ((1, 4),))
    norm_gain = jnp.clip(1.0 + 0.18 * jax.random.normal(key_of[14], (INNER,), jnp.float32), 0.1, 1.9)
    w_out = bell_draw(key_of[15], (INNER, D), INNER ** -0.5, 0.09375, ((0, 4),))
    return {"hidden": hidden, "parent": parent, "ssm_state": ssm_state, "conv_x": conv_x, "conv_bc": conv_bc, "w_gate": w_gate, "w_x": w_x, "w_bc": w_bc, "w_dt": w_dt, "dt_bias": dt_bias, "a_log": a_log, "d_skip": d_skip, "conv_wx": conv_wx, "conv_wbc": conv_wbc, "norm_gain": norm_gain, "w_out": w_out}


def reference(hidden, parent, ssm_state, conv_x, conv_bc, w_gate, w_x, w_bc, w_dt, dt_bias, a_log, d_skip, conv_wx, conv_wbc, norm_gain, w_out):
    row_ids = jnp.arange(ROWS, dtype=jnp.int32)
    source = (row_ids // BEAMS * BEAMS + parent).astype(jnp.int32)
    prior_cx = jnp.take(conv_x, source, axis=0)
    prior_cbc = jnp.take(conv_bc, source, axis=0)
    gate = jnp.dot(hidden, w_gate, preferred_element_type=jnp.float32)
    dt_raw = jnp.dot(hidden, w_dt, preferred_element_type=jnp.float32)
    xin = jnp.dot(hidden, w_x, preferred_element_type=jnp.float32).astype(jnp.bfloat16)
    bcin = jnp.dot(hidden, w_bc, preferred_element_type=jnp.float32).astype(jnp.bfloat16)
    window_x = jnp.concatenate([prior_cx, xin[:, None, :]], axis=1)
    window_bc = jnp.concatenate([prior_cbc, bcin[:, None, :]], axis=1)
    xconv = jax.nn.silu(jnp.einsum('rkc,kc->rc', window_x.astype(jnp.float32), conv_wx.astype(jnp.float32)))
    bconv = jax.nn.silu(jnp.einsum('rkc,kc->rc', window_bc.astype(jnp.float32), conv_wbc.astype(jnp.float32))).astype(jnp.bfloat16)
    bmap = bconv[:, :STATE].astype(jnp.float32)
    cmap = bconv[:, STATE:].astype(jnp.float32)
    dt = jax.nn.softplus(dt_raw + dt_bias)
    decay = jnp.exp(-dt * jnp.exp(a_log))
    xheads = xconv.reshape(ROWS, HEADS, HEAD_DIM)

    def one_head(head):
        block = lax.dynamic_index_in_dim(ssm_state, head, 1, keepdims=False)
        block = jnp.take(block, source, axis=0).astype(jnp.float32)
        x_head = lax.dynamic_index_in_dim(xheads, head, 1, keepdims=False)
        decay_head = lax.dynamic_index_in_dim(decay, head, 1, keepdims=False)
        dt_head = lax.dynamic_index_in_dim(dt, head, 1, keepdims=False)
        skip_head = lax.dynamic_index_in_dim(d_skip, head, 0, keepdims=False)
        state = decay_head[:, None, None] * block + (dt_head[:, None] * x_head)[:, :, None] * bmap[:, None, :]
        y_head = jnp.einsum('rpn,rn->rp', state, cmap) + skip_head * x_head
        return (state.astype(jnp.bfloat16), y_head)
    states, outputs = lax.map(one_head, jnp.arange(HEADS, dtype=jnp.int32))
    new_state = jnp.moveaxis(states, 0, 1)
    y_all = jnp.moveaxis(outputs, 0, 1).reshape(ROWS, INNER)
    gated = y_all * jax.nn.silu(gate)
    mean_sq = lax.optimization_barrier(jnp.mean(gated * gated, axis=1))
    scaled = (gated * lax.rsqrt(mean_sq + 1e-05)[:, None] * norm_gain).astype(jnp.bfloat16)
    mixed = jnp.dot(scaled, w_out, preferred_element_type=jnp.float32).astype(jnp.bfloat16)
    return (mixed, new_state, window_x[:, 1:], window_bc[:, 1:])
```

```python
import functools

import jax
import jax.numpy as jnp
from jax import lax
from jax.experimental import pallas as pl
from jax.experimental.pallas import tpu as pltpu
from jax.sharding import PartitionSpec as P

SPAN = 2
CHUNKS = 8
MESH = pl.DeviceIdType.MESH
F32 = jnp.float32
BF16 = jnp.bfloat16
NT = (((1,), (1,)), ((), ()))
NN = (((1,), (0,)), ((), ()))


def silu(v):
    return v / (1.0 + jnp.exp(-v))


def kernel(
    heads_count,
    hidden,
    parent,
    ssm_state,
    conv_x,
    conv_bc,
    w_gate,
    w_x,
    w_bc,
    w_dt,
    dt_bias,
    a_log,
    d_skip,
    conv_wx,
    conv_wbc,
    norm_gain,
    w_out,
    mixed,
    new_state,
    new_cx,
    new_cbc,
    wbc_v,
    wx_v,
    wg_v,
    wo_v,
    st_all,
    ns_v,
    win_all,
    prior_win,
    bc_all,
    cols_t,
    rs_send,
    rs_recv,
    bc_sem,
    x_sem,
    g_sem,
    o_sem,
    st_sem,
    ns_sem,
    pair_send,
    pair_recv,
    bcs_send,
    bcs_recv,
    rss_send,
    rss_recv,
):
    rows_dev, depth = hidden.shape
    heads_dev, head_dim, state_dim = ssm_state.shape[1:]
    inner = w_x.shape[1]
    bcw = w_bc.shape[1]
    out_cols = mixed.shape[1]
    taps = conv_wx.shape[0]
    inner_all = inner * heads_count
    span = depth // CHUNKS

    place = lax.axis_index("rows")
    me = lax.axis_index("heads")
    member = lax.rem(place, SPAN)
    partner = place + 1 - 2 * member
    mine = pl.ds(member * rows_dev, rows_dev)

    def peer(step):
        return lax.rem(me + step, heads_count)

    def chunk_copy(src, dst, sem, k):
        at = pl.ds(pl.multiple_of(k * span, span), span)
        return pltpu.make_async_copy(src.at[at], dst.at[at], sem.at[k])

    def out_copy(step):
        p = peer(step)
        at = pl.ds(pl.multiple_of(p * out_cols, out_cols), out_cols)
        return pltpu.make_async_copy(w_out.at[:, at], wo_v.at[step], o_sem.at[step])

    wbc_copy = pltpu.make_async_copy(w_bc, wbc_v, bc_sem)
    wbc_copy.start()
    for k in range(CHUNKS):
        chunk_copy(w_x, wx_v, x_sem, k).start()
    own_state = pltpu.make_async_copy(ssm_state, st_all.at[mine], st_sem)
    own_state.start()
    for k in range(CHUNKS):
        chunk_copy(w_gate, wg_v, g_sem, k).start()
    out_order = list(range(1, heads_count)) + [0]
    for step in out_order:
        out_copy(step).start()

    barrier = pltpu.get_barrier_semaphore()
    pl.semaphore_signal(barrier, inc=1, device_id={"rows": partner}, device_id_type=MESH)
    for step in range(1, heads_count):
        pl.semaphore_signal(barrier, inc=1, device_id={"heads": peer(step)}, device_id_type=MESH)

    for r in range(rows_dev):
        for k in range(taps - 1):
            win_all[member * rows_dev + r, k : k + 1, :inner] = conv_x[k, r : r + 1, :].astype(F32)
            win_all[member * rows_dev + r, k : k + 1, inner:] = conv_bc[k, r : r + 1, :].astype(F32)

    pl.semaphore_wait(barrier, heads_count)

    win_copy = pltpu.make_async_remote_copy(
        src_ref=win_all.at[mine],
        dst_ref=win_all.at[mine],
        send_sem=pair_send.at[0],
        recv_sem=pair_recv.at[0],
        device_id={"rows": partner},
        device_id_type=MESH,
    )
    win_copy.start()
    state_copy = pltpu.make_async_remote_copy(
        src_ref=ssm_state,
        dst_ref=st_all.at[mine],
        send_sem=pair_send.at[1],
        recv_sem=pair_recv.at[1],
        device_id={"rows": partner},
        device_id_type=MESH,
    )
    state_copy.start()

    dt_raw = lax.dot_general(hidden[...], w_dt[...], NT, preferred_element_type=F32)
    wbc_copy.wait()
    bcin = jnp.dot(hidden[...], wbc_v[...], preferred_element_type=F32).astype(BF16).astype(F32)

    win_copy.wait()
    sources = [parent[place * rows_dev + r] for r in range(rows_dev)]
    for r in range(rows_dev):
        for k in range(taps - 1):
            prior_win[k, r : r + 1, :] = win_all[sources[r], k : k + 1, :]

    def window_sum(lo, hi, fresh, taps_ref, out):
        total = fresh * taps_ref[taps - 1 : taps, :].astype(F32)
        for k in range(taps - 1):
            past = prior_win[k, :, lo:hi]
            total += past * taps_ref[k : k + 1, :].astype(F32)
            if k > 0:
                out[k - 1] = past.astype(BF16)
        out[taps - 2] = fresh.astype(BF16)
        return silu(total)

    bconv = window_sum(inner, inner + bcw, bcin, conv_wbc, new_cbc).astype(BF16).astype(F32)
    bc_all[me] = bconv

    def bc_copy(step, slot):
        return pltpu.make_async_remote_copy(
            src_ref=bc_all.at[slot],
            dst_ref=bc_all.at[slot],
            send_sem=bcs_send.at[step],
            recv_sem=bcs_recv.at[slot],
            device_id={"heads": peer(step)},
            device_id_type=MESH,
        )

    for step in range(1, heads_count):
        bc_copy(step, me).start()

    def project(src, dst, sem):
        def step(k, total):
            chunk_copy(src, dst, sem, k).wait()
            at = pl.ds(pl.multiple_of(k * span, span), span)
            return total + jnp.dot(hidden[:, at], dst[at, :], preferred_element_type=F32)

        return lax.fori_loop(0, CHUNKS, step, jnp.zeros((rows_dev, inner), F32))

    xin = project(w_x, wx_v, x_sem).astype(BF16).astype(F32)
    xconv = window_sum(0, inner, xin, conv_wx, new_cx)

    biased = dt_raw + dt_bias[...]
    dt = jnp.maximum(biased, 0.0) + jnp.log1p(jnp.exp(-jnp.abs(biased)))
    decay = jnp.exp(-dt * jnp.exp(a_log[...]))
    head_of = lax.broadcasted_iota(jnp.int32, (heads_dev, inner), 1) // head_dim
    spread = (lax.broadcasted_iota(jnp.int32, (heads_dev, inner), 0) == head_of).astype(F32)

    def per_column(v):
        return lax.dot_general(
            v, spread, NN, precision=lax.Precision.HIGHEST, preferred_element_type=F32
        )

    decay_c = per_column(decay)
    pushed = per_column(dt) * xconv
    skip_c = per_column(d_skip[...])
    cols_t[...] = jnp.transpose(jnp.concatenate([pushed, decay_c], axis=0))

    gate = project(w_gate, wg_v, g_sem)

    for step in range(1, heads_count):
        bc_copy(step, peer(step)).wait_recv()

    def maps(first):
        half = heads_count // 2
        parts = [bc_all[first * half + h] for h in range(half)]
        if bcw % 128 == 0:
            return jnp.concatenate(parts, axis=1)
        total = jnp.zeros((rows_dev, state_dim), F32)
        row = lax.broadcasted_iota(jnp.int32, (bcw, state_dim), 0)
        col = lax.broadcasted_iota(jnp.int32, (bcw, state_dim), 1)
        for h in range(half):
            place_h = (row + h * bcw == col).astype(F32)
            total += jnp.dot(parts[h], place_h, preferred_element_type=F32)
        return total

    bmap = maps(0)
    cmap = maps(1)
    cmap_b = cmap.astype(BF16)

    own_state.wait()
    state_copy.wait()
    row_of = lax.broadcasted_iota(jnp.int32, (rows_dev, inner), 0)
    carried = jnp.zeros((rows_dev, inner), F32)
    for r in range(rows_dev):
        block = st_all[sources[r]].reshape(inner, state_dim)
        seen = lax.dot_general(cmap_b, block, NT, preferred_element_type=F32)
        carried = jnp.where(row_of == r, seen, carried)
    overlap = jnp.sum(bmap * cmap, axis=1, keepdims=True)
    y = decay_c * carried + pushed * overlap + skip_c * xconv
    gated = y * silu(gate)
    squares = jnp.sum(gated * gated, axis=1, keepdims=True)
    scaled = (gated * norm_gain[...]).astype(BF16)
    squares_b = jnp.broadcast_to(squares, (rows_dev, 128))

    def rs_copy(step, slot):
        return pltpu.make_async_remote_copy(
            src_ref=rs_send.at[step],
            dst_ref=rs_recv.at[slot],
            send_sem=rss_send.at[step],
            recv_sem=rss_recv.at[slot],
            device_id={"heads": peer(step)},
            device_id_type=MESH,
        )

    for step in out_order:
        out_copy(step).wait()
        terms = jnp.dot(scaled, wo_v[step], preferred_element_type=F32)
        rs_send[step, :, :out_cols] = terms
        rs_send[step, :, out_cols:] = squares_b
        if step > 0:
            rs_copy(step, me).start()

    for r in range(rows_dev):
        b_row = bmap[r : r + 1, :]

        def one_head(h, carry, r=r, b_row=b_row):
            at = pl.ds(pl.multiple_of(h * head_dim, head_dim), head_dim)
            cols = cols_t[at, :]
            prior = st_all[sources[r], h].astype(F32)
            value = cols[:, rows_dev + r : rows_dev + r + 1] * prior + cols[:, r : r + 1] * b_row
            ns_v[r, h] = value.astype(BF16)
            return carry

        lax.fori_loop(0, heads_dev, one_head, 0)
        pltpu.make_async_copy(ns_v.at[r], new_state.at[r], ns_sem.at[r]).start()

    total = rs_send[0]
    for step in range(1, heads_count):
        rs_copy(step, peer(step)).wait_recv()
        total += rs_recv[peer(step)]
    mean_sq = total[:, out_cols : out_cols + 1] / inner_all
    mixed[...] = (total[:, :out_cols] * lax.rsqrt(mean_sq + 1e-05)).astype(BF16)

    for step in range(1, heads_count):
        bc_copy(step, me).wait_send()
        rs_copy(step, me).wait_send()
    for r in range(rows_dev):
        pltpu.make_async_copy(ns_v.at[r], new_state.at[r], ns_sem.at[r]).wait()


def on_device(
    heads_count,
    hidden,
    parent,
    ssm_state,
    conv_x,
    conv_bc,
    w_gate,
    w_x,
    w_bc,
    w_dt,
    dt_bias,
    a_log,
    d_skip,
    conv_wx,
    conv_wbc,
    norm_gain,
    w_out,
):
    rows_dev, depth = hidden.shape
    _, heads_dev, head_dim, state_dim = ssm_state.shape
    inner = w_x.shape[1]
    bcw = w_bc.shape[1]
    taps = conv_wx.shape[0]
    out_cols = w_out.shape[1] // heads_count
    vmem = pl.BlockSpec(memory_space=pltpu.VMEM)
    smem = pl.BlockSpec(memory_space=pltpu.SMEM)
    hbm = pl.BlockSpec(memory_space=pl.ANY)
    dma = pltpu.SemaphoreType.DMA
    sds = jax.ShapeDtypeStruct
    mixed, new_state, new_cx, new_cbc = pl.pallas_call(
        functools.partial(kernel, heads_count),
        out_shape=(
            sds((rows_dev, out_cols), BF16),
            sds(ssm_state.shape, BF16),
            sds((taps - 1, rows_dev, inner), BF16),
            sds((taps - 1, rows_dev, bcw), BF16),
        ),
        in_specs=[vmem, smem, hbm, vmem, vmem, hbm, hbm, hbm] + [vmem] * 7 + [hbm],
        out_specs=(vmem, hbm, vmem, vmem),
        scratch_shapes=[
            pltpu.VMEM((depth, bcw), BF16),
            pltpu.VMEM((depth, inner), BF16),
            pltpu.VMEM((depth, inner), BF16),
            pltpu.VMEM((heads_count, inner, out_cols), BF16),
            pltpu.VMEM((SPAN * rows_dev, heads_dev, head_dim, state_dim), BF16),
            pltpu.VMEM(ssm_state.shape, BF16),
            pltpu.VMEM((SPAN * rows_dev, taps - 1, inner + bcw), F32),
            pltpu.VMEM((taps - 1, rows_dev, inner + bcw), F32),
            pltpu.VMEM((heads_count, rows_dev, bcw), F32),
            pltpu.VMEM((inner, 2 * rows_dev), F32),
            pltpu.VMEM((heads_count, rows_dev, out_cols + 128), F32),
            pltpu.VMEM((heads_count, rows_dev, out_cols + 128), F32),
            dma,
            dma((CHUNKS,)),
            dma((CHUNKS,)),
            dma((heads_count,)),
            dma,
            dma((rows_dev,)),
            dma((2,)),
            dma((2,)),
            dma((heads_count,)),
            dma((heads_count,)),
            dma((heads_count,)),
            dma((heads_count,)),
        ],
        compiler_params=pltpu.CompilerParams(
            collective_id=0, has_side_effects=True, vmem_limit_bytes=48 * 1024 * 1024
        ),
    )(
        hidden,
        parent,
        ssm_state,
        jnp.transpose(conv_x, (1, 0, 2)),
        jnp.transpose(conv_bc, (1, 0, 2)),
        w_gate,
        w_x,
        w_bc,
        jnp.transpose(w_dt),
        dt_bias.reshape(1, -1),
        a_log.reshape(1, -1),
        d_skip.reshape(1, -1),
        conv_wx,
        conv_wbc,
        norm_gain.reshape(1, -1),
        w_out,
    )
    return (
        mixed,
        new_state,
        jnp.transpose(new_cx, (1, 0, 2)),
        jnp.transpose(new_cbc, (1, 0, 2)),
    )


def solution(mesh):
    in_specs = (
        P(("groups", "rows"), None),
        P("groups"),
        P(("groups", "rows"), "heads", None, None),
        P(("groups", "rows"), None, "heads"),
        P(("groups", "rows"), None, "heads"),
        P(None, "heads"),
        P(None, "heads"),
        P(None, "heads"),
        P(None, "heads"),
        P("heads"),
        P("heads"),
        P("heads"),
        P(None, "heads"),
        P(None, "heads"),
        P("heads"),
        P("heads", None),
    )
    out_specs = (
        P(("groups", "rows"), "heads"),
        P(("groups", "rows"), "heads", None, None),
        P(("groups", "rows"), None, "heads"),
        P(("groups", "rows"), None, "heads"),
    )
    return jax.shard_map(
        functools.partial(on_device, mesh.shape["heads"]),
        mesh=mesh,
        in_specs=in_specs,
        out_specs=out_specs,
        check_vma=False,
    )
```

```python
import functools

import jax
import jax.numpy as jnp
from jax import lax
from jax.experimental import pallas as pl
from jax.experimental.pallas import tpu as pltpu
from jax.sharding import PartitionSpec as P

SPAN = 2
CHUNKS = 8
MESH = pl.DeviceIdType.MESH
F32 = jnp.float32
BF16 = jnp.bfloat16
NT = (((1,), (1,)), ((), ()))
NN = (((1,), (0,)), ((), ()))


def silu(v):
    return v / (1.0 + jnp.exp(-v))


def kernel(
    heads_count,
    hidden_hbm,
    parent_hbm,
    ssm_state,
    conv_x_hbm,
    conv_bc_hbm,
    w_gate,
    w_x,
    w_bc,
    w_dt_hbm,
    dt_bias_hbm,
    a_log_hbm,
    d_skip_hbm,
    conv_wx_hbm,
    conv_wbc_hbm,
    norm_gain_hbm,
    w_out,
    mixed,
    new_state,
    new_cx,
    new_cbc,
    hidden,
    conv_x,
    conv_bc,
    w_dt,
    dt_bias,
    a_log,
    d_skip,
    conv_wx,
    conv_wbc,
    norm_gain,
    parent,
    in_sem,
    wbc_v,
    wx_v,
    wg_v,
    wo_v,
    st_all,
    ns_v,
    win_all,
    prior_win,
    bc_all,
    cols_t,
    rs_send,
    rs_recv,
    bc_sem,
    x_sem,
    g_sem,
    o_sem,
    st_sem,
    ns_sem,
    pair_send,
    pair_recv,
    bcs_send,
    bcs_recv,
    rss_send,
    rss_recv,
):
    rows_dev, depth = hidden.shape
    heads_dev, head_dim, state_dim = ssm_state.shape[1:]
    inner = w_x.shape[1]
    bcw = w_bc.shape[1]
    out_cols = mixed.shape[1]
    taps = conv_wx.shape[0]
    inner_all = inner * heads_count
    span = depth // CHUNKS

    place = lax.axis_index("rows")
    me = lax.axis_index("heads")
    member = lax.rem(place, SPAN)
    partner = place + 1 - 2 * member
    mine = pl.ds(member * rows_dev, rows_dev)

    def peer(step):
        return lax.rem(me + step, heads_count)

    def chunk_copy(src, dst, sem, k):
        at = pl.ds(pl.multiple_of(k * span, span), span)
        return pltpu.make_async_copy(src.at[at], dst.at[at], sem.at[k])

    def out_copy(step):
        p = peer(step)
        at = pl.ds(pl.multiple_of(p * out_cols, out_cols), out_cols)
        return pltpu.make_async_copy(w_out.at[:, at], wo_v.at[step], o_sem.at[step])

    small = (
        (hidden_hbm, hidden),
        (conv_x_hbm, conv_x),
        (conv_bc_hbm, conv_bc),
        (w_dt_hbm, w_dt),
        (dt_bias_hbm, dt_bias),
        (a_log_hbm, a_log),
        (d_skip_hbm, d_skip),
        (conv_wx_hbm, conv_wx),
        (conv_wbc_hbm, conv_wbc),
        (norm_gain_hbm, norm_gain),
        (parent_hbm, parent),
    )
    loads = [pltpu.make_async_copy(a, b, in_sem.at[i]) for i, (a, b) in enumerate(small)]
    wbc_copy = pltpu.make_async_copy(w_bc, wbc_v, bc_sem)
    for i in (1, 2, 0):
        loads[i].start()
    wbc_copy.start()
    for i in range(3, len(loads)):
        loads[i].start()
    for k in range(CHUNKS):
        chunk_copy(w_x, wx_v, x_sem, k).start()
    own_state = pltpu.make_async_copy(ssm_state, st_all.at[mine], st_sem)
    own_state.start()
    for k in range(CHUNKS):
        chunk_copy(w_gate, wg_v, g_sem, k).start()
    out_order = list(range(1, heads_count)) + [0]
    for step in out_order:
        out_copy(step).start()

    barrier = pltpu.get_barrier_semaphore()
    pl.semaphore_signal(barrier, inc=1, device_id={"rows": partner}, device_id_type=MESH)
    for step in range(1, heads_count):
        pl.semaphore_signal(barrier, inc=1, device_id={"heads": peer(step)}, device_id_type=MESH)

    loads[1].wait()
    loads[2].wait()
    for r in range(rows_dev):
        for k in range(taps - 1):
            win_all[member * rows_dev + r, k : k + 1, :inner] = conv_x[k, r : r + 1, :].astype(F32)
            win_all[member * rows_dev + r, k : k + 1, inner:] = conv_bc[k, r : r + 1, :].astype(F32)

    pl.semaphore_wait(barrier, heads_count)

    win_copy = pltpu.make_async_remote_copy(
        src_ref=win_all.at[mine],
        dst_ref=win_all.at[mine],
        send_sem=pair_send.at[0],
        recv_sem=pair_recv.at[0],
        device_id={"rows": partner},
        device_id_type=MESH,
    )
    win_copy.start()
    state_copy = pltpu.make_async_remote_copy(
        src_ref=ssm_state,
        dst_ref=st_all.at[mine],
        send_sem=pair_send.at[1],
        recv_sem=pair_recv.at[1],
        device_id={"rows": partner},
        device_id_type=MESH,
    )
    state_copy.start()

    loads[0].wait()
    for load in loads[3:]:
        load.wait()
    dt_raw = lax.dot_general(hidden[...], w_dt[...], NT, preferred_element_type=F32)
    wbc_copy.wait()
    bcin = jnp.dot(hidden[...], wbc_v[...], preferred_element_type=F32).astype(BF16).astype(F32)

    win_copy.wait()
    sources = [parent[place * rows_dev + r] for r in range(rows_dev)]
    for r in range(rows_dev):
        for k in range(taps - 1):
            prior_win[k, r : r + 1, :] = win_all[sources[r], k : k + 1, :]

    def window_sum(lo, hi, fresh, taps_ref, out):
        total = fresh * taps_ref[taps - 1 : taps, :].astype(F32)
        for k in range(taps - 1):
            past = prior_win[k, :, lo:hi]
            total += past * taps_ref[k : k + 1, :].astype(F32)
            if k > 0:
                out[k - 1] = past.astype(BF16)
        out[taps - 2] = fresh.astype(BF16)
        return silu(total)

    bconv = window_sum(inner, inner + bcw, bcin, conv_wbc, new_cbc).astype(BF16).astype(F32)
    bc_all[me] = bconv

    def bc_copy(step, slot):
        return pltpu.make_async_remote_copy(
            src_ref=bc_all.at[slot],
            dst_ref=bc_all.at[slot],
            send_sem=bcs_send.at[step],
            recv_sem=bcs_recv.at[slot],
            device_id={"heads": peer(step)},
            device_id_type=MESH,
        )

    for step in range(1, heads_count):
        bc_copy(step, me).start()

    def project(src, dst, sem):
        def step(k, total):
            chunk_copy(src, dst, sem, k).wait()
            at = pl.ds(pl.multiple_of(k * span, span), span)
            return total + jnp.dot(hidden[:, at], dst[at, :], preferred_element_type=F32)

        return lax.fori_loop(0, CHUNKS, step, jnp.zeros((rows_dev, inner), F32))

    xin = project(w_x, wx_v, x_sem).astype(BF16).astype(F32)
    xconv = window_sum(0, inner, xin, conv_wx, new_cx)

    biased = dt_raw + dt_bias[...]
    dt = jnp.maximum(biased, 0.0) + jnp.log1p(jnp.exp(-jnp.abs(biased)))
    decay = jnp.exp(-dt * jnp.exp(a_log[...]))
    head_of = lax.broadcasted_iota(jnp.int32, (heads_dev, inner), 1) // head_dim
    spread = (lax.broadcasted_iota(jnp.int32, (heads_dev, inner), 0) == head_of).astype(F32)

    def per_column(v):
        return lax.dot_general(
            v, spread, NN, precision=lax.Precision.HIGHEST, preferred_element_type=F32
        )

    decay_c = per_column(decay)
    pushed = per_column(dt) * xconv
    skip_c = per_column(d_skip[...])
    cols_t[...] = jnp.transpose(jnp.concatenate([pushed, decay_c], axis=0))

    gate = project(w_gate, wg_v, g_sem)

    for step in range(1, heads_count):
        bc_copy(step, peer(step)).wait_recv()

    def maps(first):
        half = heads_count // 2
        parts = [bc_all[first * half + h] for h in range(half)]
        if bcw % 128 == 0:
            return jnp.concatenate(parts, axis=1)
        total = jnp.zeros((rows_dev, state_dim), F32)
        row = lax.broadcasted_iota(jnp.int32, (bcw, state_dim), 0)
        col = lax.broadcasted_iota(jnp.int32, (bcw, state_dim), 1)
        for h in range(half):
            place_h = (row + h * bcw == col).astype(F32)
            total += jnp.dot(parts[h], place_h, preferred_element_type=F32)
        return total

    bmap = maps(0)
    cmap = maps(1)
    cmap_b = cmap.astype(BF16)

    own_state.wait()
    state_copy.wait()
    row_of = lax.broadcasted_iota(jnp.int32, (rows_dev, inner), 0)
    carried = jnp.zeros((rows_dev, inner), F32)
    for r in range(rows_dev):
        block = st_all[sources[r]].reshape(inner, state_dim)
        seen = lax.dot_general(cmap_b, block, NT, preferred_element_type=F32)
        carried = jnp.where(row_of == r, seen, carried)
    overlap = jnp.sum(bmap * cmap, axis=1, keepdims=True)
    y = decay_c * carried + pushed * overlap + skip_c * xconv
    gated = y * silu(gate)
    squares = jnp.sum(gated * gated, axis=1, keepdims=True)
    scaled = (gated * norm_gain[...]).astype(BF16)
    squares_b = jnp.broadcast_to(squares, (rows_dev, 128))

    def rs_copy(step, slot):
        return pltpu.make_async_remote_copy(
            src_ref=rs_send.at[step],
            dst_ref=rs_recv.at[slot],
            send_sem=rss_send.at[step],
            recv_sem=rss_recv.at[slot],
            device_id={"heads": peer(step)},
            device_id_type=MESH,
        )

    for step in out_order:
        out_copy(step).wait()
        terms = jnp.dot(scaled, wo_v[step], preferred_element_type=F32)
        rs_send[step, :, :out_cols] = terms
        rs_send[step, :, out_cols:] = squares_b
        if step > 0:
            rs_copy(step, me).start()

    for r in range(rows_dev):
        b_row = bmap[r : r + 1, :]

        def one_head(h, carry, r=r, b_row=b_row):
            at = pl.ds(pl.multiple_of(h * head_dim, head_dim), head_dim)
            cols = cols_t[at, :]
            prior = st_all[sources[r], h].astype(F32)
            value = cols[:, rows_dev + r : rows_dev + r + 1] * prior + cols[:, r : r + 1] * b_row
            ns_v[r, h] = value.astype(BF16)
            return carry

        lax.fori_loop(0, heads_dev, one_head, 0)
        pltpu.make_async_copy(ns_v.at[r], new_state.at[r], ns_sem.at[r]).start()

    total = rs_send[0]
    for step in range(1, heads_count):
        rs_copy(step, peer(step)).wait_recv()
        total += rs_recv[peer(step)]
    mean_sq = total[:, out_cols : out_cols + 1] / inner_all
    mixed[...] = (total[:, :out_cols] * lax.rsqrt(mean_sq + 1e-05)).astype(BF16)

    for step in range(1, heads_count):
        bc_copy(step, me).wait_send()
        rs_copy(step, me).wait_send()
    for r in range(rows_dev):
        pltpu.make_async_copy(ns_v.at[r], new_state.at[r], ns_sem.at[r]).wait()


def store_kernel(*refs):
    sem = refs[8]
    copies = [pltpu.make_async_copy(refs[i], refs[4 + i], sem.at[i]) for i in (1, 0, 2, 3)]
    for copy in copies:
        copy.start()
    for copy in copies:
        copy.wait()


def on_device(
    heads_count,
    hidden,
    parent,
    ssm_state,
    conv_x,
    conv_bc,
    w_gate,
    w_x,
    w_bc,
    w_dt,
    dt_bias,
    a_log,
    d_skip,
    conv_wx,
    conv_wbc,
    norm_gain,
    w_out,
):
    rows_dev, depth = hidden.shape
    _, heads_dev, head_dim, state_dim = ssm_state.shape
    inner = w_x.shape[1]
    bcw = w_bc.shape[1]
    taps = conv_wx.shape[0]
    out_cols = w_out.shape[1] // heads_count
    vmem = pl.BlockSpec(memory_space=pltpu.VMEM)
    hbm = pl.BlockSpec(memory_space=pltpu.HBM)
    dma = pltpu.SemaphoreType.DMA
    sds = jax.ShapeDtypeStruct
    results = pl.pallas_call(
        functools.partial(kernel, heads_count),
        out_shape=(
            sds((rows_dev, out_cols), BF16),
            sds(ssm_state.shape, BF16),
            sds((taps - 1, rows_dev, inner), BF16),
            sds((taps - 1, rows_dev, bcw), BF16),
        ),
        in_specs=[hbm] * 16,
        out_specs=(vmem, hbm, vmem, vmem),
        scratch_shapes=[
            pltpu.VMEM(hidden.shape, BF16),
            pltpu.VMEM((taps - 1, rows_dev, inner), BF16),
            pltpu.VMEM((taps - 1, rows_dev, bcw), BF16),
            pltpu.VMEM((heads_dev, depth), BF16),
            pltpu.VMEM((1, heads_dev), F32),
            pltpu.VMEM((1, heads_dev), F32),
            pltpu.VMEM((1, heads_dev), F32),
            pltpu.VMEM(conv_wx.shape, BF16),
            pltpu.VMEM(conv_wbc.shape, BF16),
            pltpu.VMEM((1, inner), F32),
            pltpu.SMEM(parent.shape, jnp.int32),
            dma((11,)),
            pltpu.VMEM((depth, bcw), BF16),
            pltpu.VMEM((depth, inner), BF16),
            pltpu.VMEM((depth, inner), BF16),
            pltpu.VMEM((heads_count, inner, out_cols), BF16),
            pltpu.VMEM((SPAN * rows_dev, heads_dev, head_dim, state_dim), BF16),
            pltpu.VMEM(ssm_state.shape, BF16),
            pltpu.VMEM((SPAN * rows_dev, taps - 1, inner + bcw), F32),
            pltpu.VMEM((taps - 1, rows_dev, inner + bcw), F32),
            pltpu.VMEM((heads_count, rows_dev, bcw), F32),
            pltpu.VMEM((inner, 2 * rows_dev), F32),
            pltpu.VMEM((heads_count, rows_dev, out_cols + 128), F32),
            pltpu.VMEM((heads_count, rows_dev, out_cols + 128), F32),
            dma,
            dma((CHUNKS,)),
            dma((CHUNKS,)),
            dma((heads_count,)),
            dma,
            dma((rows_dev,)),
            dma((2,)),
            dma((2,)),
            dma((heads_count,)),
            dma((heads_count,)),
            dma((heads_count,)),
            dma((heads_count,)),
        ],
        compiler_params=pltpu.CompilerParams(
            collective_id=0, has_side_effects=True, vmem_limit_bytes=60 * 1024 * 1024
        ),
    )(
        hidden,
        parent,
        ssm_state,
        jnp.transpose(conv_x, (1, 0, 2)),
        jnp.transpose(conv_bc, (1, 0, 2)),
        w_gate,
        w_x,
        w_bc,
        jnp.transpose(w_dt),
        dt_bias.reshape(1, -1),
        a_log.reshape(1, -1),
        d_skip.reshape(1, -1),
        conv_wx,
        conv_wbc,
        norm_gain.reshape(1, -1),
        w_out,
    )
    mixed, new_state, new_cx, new_cbc = pl.pallas_call(
        store_kernel,
        out_shape=tuple(sds(v.shape, v.dtype) for v in results),
        in_specs=[pl.BlockSpec(memory_space=pl.ANY)] * 4,
        out_specs=(hbm,) * 4,
        scratch_shapes=[dma((4,))],
    )(*results)
    return (
        mixed,
        new_state,
        jnp.transpose(new_cx, (1, 0, 2)),
        jnp.transpose(new_cbc, (1, 0, 2)),
    )


def solution(mesh):
    in_specs = (
        P(("groups", "rows"), None),
        P("groups"),
        P(("groups", "rows"), "heads", None, None),
        P(("groups", "rows"), None, "heads"),
        P(("groups", "rows"), None, "heads"),
        P(None, "heads"),
        P(None, "heads"),
        P(None, "heads"),
        P(None, "heads"),
        P("heads"),
        P("heads"),
        P("heads"),
        P(None, "heads"),
        P(None, "heads"),
        P("heads"),
        P("heads", None),
    )
    out_specs = (
        P(("groups", "rows"), "heads"),
        P(("groups", "rows"), "heads", None, None),
        P(("groups", "rows"), None, "heads"),
        P(("groups", "rows"), None, "heads"),
    )
    return jax.shard_map(
        functools.partial(on_device, mesh.shape["heads"]),
        mesh=mesh,
        in_specs=in_specs,
        out_specs=out_specs,
        check_vma=False,
    )
```

```python
import functools

import jax
import jax.numpy as jnp
from jax import lax
from jax.experimental import pallas as pl
from jax.experimental.pallas import tpu as pltpu
from jax.sharding import PartitionSpec as P

SPAN = 2
CHUNKS = 8
MESH = pl.DeviceIdType.MESH
F32 = jnp.float32
BF16 = jnp.bfloat16
NT = (((1,), (1,)), ((), ()))
NN = (((1,), (0,)), ((), ()))


def silu(v):
    return v / (1.0 + jnp.exp(-v))


def kernel(
    heads_count,
    hidden_hbm,
    parent_hbm,
    ssm_state,
    conv_x_hbm,
    conv_bc_hbm,
    w_gate,
    w_x,
    w_bc,
    w_dt_hbm,
    dt_bias_hbm,
    a_log_hbm,
    d_skip_hbm,
    conv_wx_hbm,
    conv_wbc_hbm,
    norm_gain_hbm,
    w_out,
    mixed,
    new_state,
    new_cx,
    new_cbc,
    hidden,
    conv_x,
    conv_bc,
    w_dt,
    dt_bias,
    a_log,
    d_skip,
    conv_wx,
    conv_wbc,
    norm_gain,
    parent,
    in_sem,
    wbc_v,
    wx_v,
    wg_v,
    wo_v,
    st_all,
    ns_v,
    win_all,
    prior_win,
    bc_all,
    cols_t,
    rs_send,
    rs_recv,
    bc_sem,
    x_sem,
    g_sem,
    o_sem,
    st_sem,
    ns_sem,
    pair_send,
    pair_recv,
    bcs_send,
    bcs_recv,
    rss_send,
    rss_recv,
):
    rows_dev, depth = hidden.shape
    heads_dev, head_dim, state_dim = ssm_state.shape[1:]
    inner = w_x.shape[1]
    bcw = w_bc.shape[1]
    out_cols = mixed.shape[1]
    taps = conv_wx.shape[0]
    inner_all = inner * heads_count
    span = depth // CHUNKS

    place = lax.axis_index("rows")
    me = lax.axis_index("heads")
    member = lax.rem(place, SPAN)
    partner = place + 1 - 2 * member
    mine = pl.ds(member * rows_dev, rows_dev)

    def peer(step):
        return lax.rem(me + step, heads_count)

    def chunk_copy(src, dst, sem, k):
        at = pl.ds(pl.multiple_of(k * span, span), span)
        return pltpu.make_async_copy(src.at[at], dst.at[at], sem.at[k])

    def out_copy(step):
        p = peer(step)
        at = pl.ds(pl.multiple_of(p * out_cols, out_cols), out_cols)
        return pltpu.make_async_copy(w_out.at[:, at], wo_v.at[step], o_sem.at[step])

    small = (
        (hidden_hbm, hidden),
        (conv_x_hbm, conv_x),
        (conv_bc_hbm, conv_bc),
        (w_dt_hbm, w_dt),
        (dt_bias_hbm, dt_bias),
        (a_log_hbm, a_log),
        (d_skip_hbm, d_skip),
        (conv_wx_hbm, conv_wx),
        (conv_wbc_hbm, conv_wbc),
        (norm_gain_hbm, norm_gain),
        (parent_hbm, parent),
    )
    loads = [pltpu.make_async_copy(a, b, in_sem.at[i]) for i, (a, b) in enumerate(small)]
    wbc_copy = pltpu.make_async_copy(w_bc, wbc_v, bc_sem)
    for i in (1, 2, 0):
        loads[i].start()
    wbc_copy.start()
    for i in range(3, len(loads)):
        loads[i].start()
    for k in range(CHUNKS):
        chunk_copy(w_x, wx_v, x_sem, k).start()
    own_state = pltpu.make_async_copy(ssm_state, st_all.at[mine], st_sem)
    own_state.start()
    for k in range(CHUNKS):
        chunk_copy(w_gate, wg_v, g_sem, k).start()
    out_order = list(range(1, heads_count)) + [0]
    for step in out_order:
        out_copy(step).start()

    barrier = pltpu.get_barrier_semaphore()
    pl.semaphore_signal(barrier, inc=1, device_id={"rows": partner}, device_id_type=MESH)
    for step in range(1, heads_count):
        pl.semaphore_signal(barrier, inc=1, device_id={"heads": peer(step)}, device_id_type=MESH)

    loads[1].wait()
    loads[2].wait()
    for r in range(rows_dev):
        for k in range(taps - 1):
            win_all[member * rows_dev + r, k : k + 1, :inner] = conv_x[k, r : r + 1, :].astype(F32)
            win_all[member * rows_dev + r, k : k + 1, inner:] = conv_bc[k, r : r + 1, :].astype(F32)

    pl.semaphore_wait(barrier, heads_count)

    win_copy = pltpu.make_async_remote_copy(
        src_ref=win_all.at[mine],
        dst_ref=win_all.at[mine],
        send_sem=pair_send.at[0],
        recv_sem=pair_recv.at[0],
        device_id={"rows": partner},
        device_id_type=MESH,
    )
    win_copy.start()
    state_copy = pltpu.make_async_remote_copy(
        src_ref=ssm_state,
        dst_ref=st_all.at[mine],
        send_sem=pair_send.at[1],
        recv_sem=pair_recv.at[1],
        device_id={"rows": partner},
        device_id_type=MESH,
    )
    state_copy.start()

    loads[0].wait()
    for load in loads[3:]:
        load.wait()
    dt_raw = lax.dot_general(hidden[...], w_dt[...], NT, preferred_element_type=F32)
    wbc_copy.wait()
    bcin = jnp.dot(hidden[...], wbc_v[...], preferred_element_type=F32).astype(BF16).astype(F32)

    win_copy.wait()
    sources = [parent[place * rows_dev + r] for r in range(rows_dev)]
    for r in range(rows_dev):
        for k in range(taps - 1):
            prior_win[k, r : r + 1, :] = win_all[sources[r], k : k + 1, :]

    def window_sum(lo, hi, fresh, taps_ref, out):
        total = fresh * taps_ref[taps - 1 : taps, :].astype(F32)
        for k in range(taps - 1):
            past = prior_win[k, :, lo:hi]
            total += past * taps_ref[k : k + 1, :].astype(F32)
            if k > 0:
                out[k - 1] = past.astype(BF16)
        out[taps - 2] = fresh.astype(BF16)
        return silu(total)

    bconv = window_sum(inner, inner + bcw, bcin, conv_wbc, new_cbc).astype(BF16).astype(F32)
    bc_all[me] = bconv

    def bc_copy(step, slot):
        return pltpu.make_async_remote_copy(
            src_ref=bc_all.at[slot],
            dst_ref=bc_all.at[slot],
            send_sem=bcs_send.at[step],
            recv_sem=bcs_recv.at[slot],
            device_id={"heads": peer(step)},
            device_id_type=MESH,
        )

    for step in range(1, heads_count):
        bc_copy(step, me).start()

    def project(src, dst, sem):
        def step(k, total):
            chunk_copy(src, dst, sem, k).wait()
            at = pl.ds(pl.multiple_of(k * span, span), span)
            return total + jnp.dot(hidden[:, at], dst[at, :], preferred_element_type=F32)

        return lax.fori_loop(0, CHUNKS, step, jnp.zeros((rows_dev, inner), F32))

    xin = project(w_x, wx_v, x_sem).astype(BF16).astype(F32)
    xconv = window_sum(0, inner, xin, conv_wx, new_cx)

    biased = dt_raw + dt_bias[...]
    dt = jnp.maximum(biased, 0.0) + jnp.log1p(jnp.exp(-jnp.abs(biased)))
    decay = jnp.exp(-dt * jnp.exp(a_log[...]))
    head_of = lax.broadcasted_iota(jnp.int32, (heads_dev, inner), 1) // head_dim
    spread = (lax.broadcasted_iota(jnp.int32, (heads_dev, inner), 0) == head_of).astype(F32)

    def per_column(v):
        return lax.dot_general(
            v, spread, NN, precision=lax.Precision.HIGHEST, preferred_element_type=F32
        )

    decay_c = per_column(decay)
    pushed = per_column(dt) * xconv
    skip_c = per_column(d_skip[...])
    cols_t[...] = jnp.transpose(jnp.concatenate([pushed, decay_c], axis=0))

    gate = project(w_gate, wg_v, g_sem)

    for step in range(1, heads_count):
        bc_copy(step, peer(step)).wait_recv()

    def maps(first):
        half = heads_count // 2
        parts = [bc_all[first * half + h] for h in range(half)]
        if bcw % 128 == 0:
            return jnp.concatenate(parts, axis=1)
        total = jnp.zeros((rows_dev, state_dim), F32)
        row = lax.broadcasted_iota(jnp.int32, (bcw, state_dim), 0)
        col = lax.broadcasted_iota(jnp.int32, (bcw, state_dim), 1)
        for h in range(half):
            place_h = (row + h * bcw == col).astype(F32)
            total += jnp.dot(parts[h], place_h, preferred_element_type=F32)
        return total

    bmap = maps(0)
    cmap = maps(1)
    cmap_b = cmap.astype(BF16)

    own_state.wait()
    state_copy.wait()
    row_of = lax.broadcasted_iota(jnp.int32, (rows_dev, inner), 0)
    carried = jnp.zeros((rows_dev, inner), F32)
    for r in range(rows_dev):
        block = st_all[sources[r]].reshape(inner, state_dim)
        seen = lax.dot_general(cmap_b, block, NT, preferred_element_type=F32)
        carried = jnp.where(row_of == r, seen, carried)
    overlap = jnp.sum(bmap * cmap, axis=1, keepdims=True)
    y = decay_c * carried + pushed * overlap + skip_c * xconv
    gated = y * silu(gate)
    squares = jnp.sum(gated * gated, axis=1, keepdims=True)
    scaled = (gated * norm_gain[...]).astype(BF16)
    squares_b = jnp.broadcast_to(squares, (rows_dev, 128))

    def rs_copy(step, slot):
        return pltpu.make_async_remote_copy(
            src_ref=rs_send.at[step],
            dst_ref=rs_recv.at[slot],
            send_sem=rss_send.at[step],
            recv_sem=rss_recv.at[slot],
            device_id={"heads": peer(step)},
            device_id_type=MESH,
        )

    for step in out_order:
        out_copy(step).wait()
        terms = jnp.dot(scaled, wo_v[step], preferred_element_type=F32)
        rs_send[step, :, :out_cols] = terms
        rs_send[step, :, out_cols:] = squares_b
        if step > 0:
            rs_copy(step, me).start()

    for r in range(rows_dev):
        b_row = bmap[r : r + 1, :]

        def one_head(h, carry, r=r, b_row=b_row):
            at = pl.ds(pl.multiple_of(h * head_dim, head_dim), head_dim)
            cols = cols_t[at, :]
            prior = st_all[sources[r], h].astype(F32)
            value = cols[:, rows_dev + r : rows_dev + r + 1] * prior + cols[:, r : r + 1] * b_row
            ns_v[r, h] = value.astype(BF16)
            return carry

        lax.fori_loop(0, heads_dev, one_head, 0)
        pltpu.make_async_copy(ns_v.at[r], new_state.at[r], ns_sem.at[r]).start()

    total = rs_send[0]
    for step in range(1, heads_count):
        rs_copy(step, peer(step)).wait_recv()
        total += rs_recv[peer(step)]
    mean_sq = total[:, out_cols : out_cols + 1] / inner_all
    mixed[...] = (total[:, :out_cols] * lax.rsqrt(mean_sq + 1e-05)).astype(BF16)

    for step in range(1, heads_count):
        bc_copy(step, me).wait_send()
        rs_copy(step, me).wait_send()
    for r in range(rows_dev):
        pltpu.make_async_copy(ns_v.at[r], new_state.at[r], ns_sem.at[r]).wait()


def store_kernel(*refs):
    ins, outs, held = refs[:4], refs[4:8], refs[8:12]
    in_sem, out_sem = refs[12:]
    rows_dev = ins[1].shape[0]
    loads = [pltpu.make_async_copy(ins[1].at[r], held[1].at[r], in_sem.at[r]) for r in range(rows_dev)]
    stores = [pltpu.make_async_copy(held[1].at[r], outs[1].at[r], out_sem.at[r]) for r in range(rows_dev)]
    for n, i in enumerate((0, 2, 3)):
        loads.append(pltpu.make_async_copy(ins[i], held[i], in_sem.at[rows_dev + n]))
        stores.append(pltpu.make_async_copy(held[i], outs[i], out_sem.at[rows_dev + n]))
    for load in loads:
        load.start()
    for load, store in zip(loads, stores):
        load.wait()
        store.start()
    for store in stores:
        store.wait()


def on_device(
    heads_count,
    hidden,
    parent,
    ssm_state,
    conv_x,
    conv_bc,
    w_gate,
    w_x,
    w_bc,
    w_dt,
    dt_bias,
    a_log,
    d_skip,
    conv_wx,
    conv_wbc,
    norm_gain,
    w_out,
):
    rows_dev, depth = hidden.shape
    _, heads_dev, head_dim, state_dim = ssm_state.shape
    inner = w_x.shape[1]
    bcw = w_bc.shape[1]
    taps = conv_wx.shape[0]
    out_cols = w_out.shape[1] // heads_count
    vmem = pl.BlockSpec(memory_space=pltpu.VMEM)
    hbm = pl.BlockSpec(memory_space=pltpu.HBM)
    dma = pltpu.SemaphoreType.DMA
    sds = jax.ShapeDtypeStruct
    results = pl.pallas_call(
        functools.partial(kernel, heads_count),
        out_shape=(
            sds((rows_dev, out_cols), BF16),
            sds(ssm_state.shape, BF16),
            sds((taps - 1, rows_dev, inner), BF16),
            sds((taps - 1, rows_dev, bcw), BF16),
        ),
        in_specs=[hbm] * 16,
        out_specs=(vmem, hbm, vmem, vmem),
        scratch_shapes=[
            pltpu.VMEM(hidden.shape, BF16),
            pltpu.VMEM((taps - 1, rows_dev, inner), BF16),
            pltpu.VMEM((taps - 1, rows_dev, bcw), BF16),
            pltpu.VMEM((heads_dev, depth), BF16),
            pltpu.VMEM((1, heads_dev), F32),
            pltpu.VMEM((1, heads_dev), F32),
            pltpu.VMEM((1, heads_dev), F32),
            pltpu.VMEM(conv_wx.shape, BF16),
            pltpu.VMEM(conv_wbc.shape, BF16),
            pltpu.VMEM((1, inner), F32),
            pltpu.SMEM(parent.shape, jnp.int32),
            dma((11,)),
            pltpu.VMEM((depth, bcw), BF16),
            pltpu.VMEM((depth, inner), BF16),
            pltpu.VMEM((depth, inner), BF16),
            pltpu.VMEM((heads_count, inner, out_cols), BF16),
            pltpu.VMEM((SPAN * rows_dev, heads_dev, head_dim, state_dim), BF16),
            pltpu.VMEM(ssm_state.shape, BF16),
            pltpu.VMEM((SPAN * rows_dev, taps - 1, inner + bcw), F32),
            pltpu.VMEM((taps - 1, rows_dev, inner + bcw), F32),
            pltpu.VMEM((heads_count, rows_dev, bcw), F32),
            pltpu.VMEM((inner, 2 * rows_dev), F32),
            pltpu.VMEM((heads_count, rows_dev, out_cols + 128), F32),
            pltpu.VMEM((heads_count, rows_dev, out_cols + 128), F32),
            dma,
            dma((CHUNKS,)),
            dma((CHUNKS,)),
            dma((heads_count,)),
            dma,
            dma((rows_dev,)),
            dma((2,)),
            dma((2,)),
            dma((heads_count,)),
            dma((heads_count,)),
            dma((heads_count,)),
            dma((heads_count,)),
        ],
        compiler_params=pltpu.CompilerParams(
            collective_id=0, has_side_effects=True, vmem_limit_bytes=60 * 1024 * 1024
        ),
    )(
        hidden,
        parent,
        ssm_state,
        jnp.transpose(conv_x, (1, 0, 2)),
        jnp.transpose(conv_bc, (1, 0, 2)),
        w_gate,
        w_x,
        w_bc,
        jnp.transpose(w_dt),
        dt_bias.reshape(1, -1),
        a_log.reshape(1, -1),
        d_skip.reshape(1, -1),
        conv_wx,
        conv_wbc,
        norm_gain.reshape(1, -1),
        w_out,
    )
    mixed, new_state, new_cx, new_cbc = pl.pallas_call(
        store_kernel,
        out_shape=tuple(sds(v.shape, v.dtype) for v in results),
        in_specs=[hbm] * 4,
        out_specs=(hbm,) * 4,
        scratch_shapes=[pltpu.VMEM(v.shape, v.dtype) for v in results]
        + [dma((rows_dev + 3,)), dma((rows_dev + 3,))],
        compiler_params=pltpu.CompilerParams(vmem_limit_bytes=60 * 1024 * 1024),
    )(*results)
    return (
        mixed,
        new_state,
        jnp.transpose(new_cx, (1, 0, 2)),
        jnp.transpose(new_cbc, (1, 0, 2)),
    )


def solution(mesh):
    in_specs = (
        P(("groups", "rows"), None),
        P("groups"),
        P(("groups", "rows"), "heads", None, None),
        P(("groups", "rows"), None, "heads"),
        P(("groups", "rows"), None, "heads"),
        P(None, "heads"),
        P(None, "heads"),
        P(None, "heads"),
        P(None, "heads"),
        P("heads"),
        P("heads"),
        P("heads"),
        P(None, "heads"),
        P(None, "heads"),
        P("heads"),
        P("heads", None),
    )
    out_specs = (
        P(("groups", "rows"), "heads"),
        P(("groups", "rows"), "heads", None, None),
        P(("groups", "rows"), None, "heads"),
        P(("groups", "rows"), None, "heads"),
    )
    return jax.shard_map(
        functools.partial(on_device, mesh.shape["heads"]),
        mesh=mesh,
        in_specs=in_specs,
        out_specs=out_specs,
        check_vma=False,
    )
```

```python
import functools

import jax
import jax.numpy as jnp
from jax import lax
from jax.experimental import pallas as pl
from jax.experimental.pallas import tpu as pltpu
from jax.sharding import PartitionSpec as P

SPAN = 2
CHUNKS = 8
MESH = pl.DeviceIdType.MESH
F32 = jnp.float32
BF16 = jnp.bfloat16
NT = (((1,), (1,)), ((), ()))
NN = (((1,), (0,)), ((), ()))


def silu(v):
    return v / (1.0 + jnp.exp(-v))


def kernel(
    heads_count,
    hidden_hbm,
    parent_hbm,
    ssm_state,
    conv_x_hbm,
    conv_bc_hbm,
    w_gate,
    w_x,
    w_bc,
    w_dt_hbm,
    dt_bias_hbm,
    a_log_hbm,
    d_skip_hbm,
    conv_wx_hbm,
    conv_wbc_hbm,
    norm_gain_hbm,
    w_out,
    mixed,
    new_state,
    new_cx,
    new_cbc,
    hidden,
    conv_x,
    conv_bc,
    w_dt,
    dt_bias,
    a_log,
    d_skip,
    conv_wx,
    conv_wbc,
    norm_gain,
    parent,
    in_sem,
    wbc_v,
    wx_v,
    wg_v,
    wo_v,
    st_all,
    ns_v,
    win_all,
    prior_win,
    bc_all,
    cols_t,
    rs_send,
    rs_recv,
    bc_sem,
    x_sem,
    g_sem,
    o_sem,
    st_sem,
    ns_sem,
    pair_send,
    pair_recv,
    bcs_send,
    bcs_recv,
    rss_send,
    rss_recv,
):
    rows_dev, depth = hidden.shape
    heads_dev, head_dim, state_dim = ssm_state.shape[1:]
    inner = w_x.shape[1]
    bcw = w_bc.shape[1]
    out_cols = mixed.shape[1]
    taps = conv_wx.shape[0]
    inner_all = inner * heads_count
    span = depth // CHUNKS

    place = lax.axis_index("rows")
    me = lax.axis_index("heads")
    member = lax.rem(place, SPAN)
    partner = place + 1 - 2 * member
    mine = pl.ds(member * rows_dev, rows_dev)

    def peer(step):
        return lax.rem(me + step, heads_count)

    def chunk_copy(src, dst, sem, k):
        at = pl.ds(pl.multiple_of(k * span, span), span)
        return pltpu.make_async_copy(src.at[at], dst.at[at], sem.at[k])

    def out_copy(step):
        p = peer(step)
        at = pl.ds(pl.multiple_of(p * out_cols, out_cols), out_cols)
        return pltpu.make_async_copy(w_out.at[:, at], wo_v.at[step], o_sem.at[step])

    small = (
        (hidden_hbm, hidden),
        (conv_x_hbm, conv_x),
        (conv_bc_hbm, conv_bc),
        (w_dt_hbm, w_dt),
        (dt_bias_hbm, dt_bias),
        (a_log_hbm, a_log),
        (d_skip_hbm, d_skip),
        (conv_wx_hbm, conv_wx),
        (conv_wbc_hbm, conv_wbc),
        (norm_gain_hbm, norm_gain),
        (parent_hbm, parent),
    )
    loads = [pltpu.make_async_copy(a, b, in_sem.at[i]) for i, (a, b) in enumerate(small)]
    wbc_copy = pltpu.make_async_copy(w_bc, wbc_v, bc_sem)
    for i in (1, 2, 0):
        loads[i].start()
    wbc_copy.start()
    for i in range(3, len(loads)):
        loads[i].start()
    for k in range(CHUNKS):
        chunk_copy(w_x, wx_v, x_sem, k).start()
    own_state = pltpu.make_async_copy(ssm_state, st_all.at[mine], st_sem)
    own_state.start()
    out_order = list(range(1, heads_count)) + [0]

    barrier = pltpu.get_barrier_semaphore()
    pl.semaphore_signal(barrier, inc=1, device_id={"rows": partner}, device_id_type=MESH)
    for step in range(1, heads_count):
        pl.semaphore_signal(barrier, inc=1, device_id={"heads": peer(step)}, device_id_type=MESH)

    loads[1].wait()
    loads[2].wait()
    for r in range(rows_dev):
        for k in range(taps - 1):
            win_all[member * rows_dev + r, k : k + 1, :inner] = conv_x[k, r : r + 1, :].astype(F32)
            win_all[member * rows_dev + r, k : k + 1, inner:] = conv_bc[k, r : r + 1, :].astype(F32)

    pl.semaphore_wait(barrier, heads_count)

    win_copy = pltpu.make_async_remote_copy(
        src_ref=win_all.at[mine],
        dst_ref=win_all.at[mine],
        send_sem=pair_send.at[0],
        recv_sem=pair_recv.at[0],
        device_id={"rows": partner},
        device_id_type=MESH,
    )
    win_copy.start()
    state_copy = pltpu.make_async_remote_copy(
        src_ref=ssm_state,
        dst_ref=st_all.at[mine],
        send_sem=pair_send.at[1],
        recv_sem=pair_recv.at[1],
        device_id={"rows": partner},
        device_id_type=MESH,
    )
    state_copy.start()
    for k in range(CHUNKS):
        chunk_copy(w_gate, wg_v, g_sem, k).start()
    for step in out_order:
        out_copy(step).start()

    loads[0].wait()
    for load in loads[3:]:
        load.wait()
    dt_raw = lax.dot_general(hidden[...], w_dt[...], NT, preferred_element_type=F32)
    wbc_copy.wait()
    bcin = jnp.dot(hidden[...], wbc_v[...], preferred_element_type=F32).astype(BF16).astype(F32)

    win_copy.wait()
    sources = [parent[place * rows_dev + r] for r in range(rows_dev)]
    for r in range(rows_dev):
        for k in range(taps - 1):
            prior_win[k, r : r + 1, :] = win_all[sources[r], k : k + 1, :]

    def window_sum(lo, hi, fresh, taps_ref, out):
        total = fresh * taps_ref[taps - 1 : taps, :].astype(F32)
        for k in range(taps - 1):
            past = prior_win[k, :, lo:hi]
            total += past * taps_ref[k : k + 1, :].astype(F32)
            if k > 0:
                out[k - 1] = past.astype(BF16)
        out[taps - 2] = fresh.astype(BF16)
        return silu(total)

    bconv = window_sum(inner, inner + bcw, bcin, conv_wbc, new_cbc).astype(BF16).astype(F32)
    bc_all[me] = bconv

    def bc_copy(step, slot):
        return pltpu.make_async_remote_copy(
            src_ref=bc_all.at[slot],
            dst_ref=bc_all.at[slot],
            send_sem=bcs_send.at[step],
            recv_sem=bcs_recv.at[slot],
            device_id={"heads": peer(step)},
            device_id_type=MESH,
        )

    for step in range(1, heads_count):
        bc_copy(step, me).start()

    def project(src, dst, sem):
        def step(k, total):
            chunk_copy(src, dst, sem, k).wait()
            at = pl.ds(pl.multiple_of(k * span, span), span)
            return total + jnp.dot(hidden[:, at], dst[at, :], preferred_element_type=F32)

        return lax.fori_loop(0, CHUNKS, step, jnp.zeros((rows_dev, inner), F32))

    xin = project(w_x, wx_v, x_sem).astype(BF16).astype(F32)
    xconv = window_sum(0, inner, xin, conv_wx, new_cx)

    biased = dt_raw + dt_bias[...]
    dt = jnp.maximum(biased, 0.0) + jnp.log1p(jnp.exp(-jnp.abs(biased)))
    decay = jnp.exp(-dt * jnp.exp(a_log[...]))
    head_of = lax.broadcasted_iota(jnp.int32, (heads_dev, inner), 1) // head_dim
    spread = (lax.broadcasted_iota(jnp.int32, (heads_dev, inner), 0) == head_of).astype(F32)

    def per_column(v):
        return lax.dot_general(
            v, spread, NN, precision=lax.Precision.HIGHEST, preferred_element_type=F32
        )

    decay_c = per_column(decay)
    pushed = per_column(dt) * xconv
    skip_c = per_column(d_skip[...])
    cols_t[...] = jnp.transpose(jnp.concatenate([pushed, decay_c], axis=0))

    for step in range(1, heads_count):
        bc_copy(step, peer(step)).wait_recv()

    def maps(first):
        half = heads_count // 2
        parts = [bc_all[first * half + h] for h in range(half)]
        if bcw % 128 == 0:
            return jnp.concatenate(parts, axis=1)
        total = jnp.zeros((rows_dev, state_dim), F32)
        row = lax.broadcasted_iota(jnp.int32, (bcw, state_dim), 0)
        col = lax.broadcasted_iota(jnp.int32, (bcw, state_dim), 1)
        for h in range(half):
            place_h = (row + h * bcw == col).astype(F32)
            total += jnp.dot(parts[h], place_h, preferred_element_type=F32)
        return total

    bmap = maps(0)
    cmap = maps(1)
    cmap_b = cmap.astype(BF16)

    own_state.wait()
    state_copy.wait()
    row_of = lax.broadcasted_iota(jnp.int32, (rows_dev, inner), 0)
    carried = jnp.zeros((rows_dev, inner), F32)
    for r in range(rows_dev):
        block = st_all[sources[r]].reshape(inner, state_dim)
        seen = lax.dot_general(cmap_b, block, NT, preferred_element_type=F32)
        carried = jnp.where(row_of == r, seen, carried)
    overlap = jnp.sum(bmap * cmap, axis=1, keepdims=True)

    def update_rows(first, last):
        for r in range(first, last):
            b_row = bmap[r : r + 1, :]

            def one_head(h, carry, r=r, b_row=b_row):
                at = pl.ds(pl.multiple_of(h * head_dim, head_dim), head_dim)
                cols = cols_t[at, :]
                prior = st_all[sources[r], h].astype(F32)
                value = cols[:, rows_dev + r : rows_dev + r + 1] * prior + cols[:, r : r + 1] * b_row
                ns_v[r, h] = value.astype(BF16)
                return carry

            lax.fori_loop(0, heads_dev, one_head, 0, unroll=2)
            pltpu.make_async_copy(ns_v.at[r], new_state.at[r], ns_sem.at[r]).start()

    early = rows_dev // 2
    update_rows(0, early)
    gate = project(w_gate, wg_v, g_sem)
    y = decay_c * carried + pushed * overlap + skip_c * xconv
    gated = y * silu(gate)
    squares = jnp.sum(gated * gated, axis=1, keepdims=True)
    scaled = (gated * norm_gain[...]).astype(BF16)
    squares_b = jnp.broadcast_to(squares, (rows_dev, 128))

    def rs_copy(step, slot):
        return pltpu.make_async_remote_copy(
            src_ref=rs_send.at[step],
            dst_ref=rs_recv.at[slot],
            send_sem=rss_send.at[step],
            recv_sem=rss_recv.at[slot],
            device_id={"heads": peer(step)},
            device_id_type=MESH,
        )

    for step in out_order:
        out_copy(step).wait()
        terms = jnp.dot(scaled, wo_v[step], preferred_element_type=F32)
        rs_send[step, :, :out_cols] = terms
        rs_send[step, :, out_cols:] = squares_b
        if step > 0:
            rs_copy(step, me).start()

    update_rows(early, rows_dev)

    total = rs_send[0]
    for step in range(1, heads_count):
        rs_copy(step, peer(step)).wait_recv()
        total += rs_recv[peer(step)]
    mean_sq = total[:, out_cols : out_cols + 1] / inner_all
    mixed[...] = (total[:, :out_cols] * lax.rsqrt(mean_sq + 1e-05)).astype(BF16)

    for step in range(1, heads_count):
        bc_copy(step, me).wait_send()
        rs_copy(step, me).wait_send()
    for r in range(rows_dev):
        pltpu.make_async_copy(ns_v.at[r], new_state.at[r], ns_sem.at[r]).wait()


def store_kernel(*refs):
    ins, outs, held = refs[:4], refs[4:8], refs[8:12]
    in_sem, out_sem = refs[12:]
    rows_dev = ins[1].shape[0]
    loads = [pltpu.make_async_copy(ins[1].at[r], held[1].at[r], in_sem.at[r]) for r in range(rows_dev)]
    stores = [pltpu.make_async_copy(held[1].at[r], outs[1].at[r], out_sem.at[r]) for r in range(rows_dev)]
    for n, i in enumerate((0, 2, 3)):
        loads.append(pltpu.make_async_copy(ins[i], held[i], in_sem.at[rows_dev + n]))
        stores.append(pltpu.make_async_copy(held[i], outs[i], out_sem.at[rows_dev + n]))
    for load in loads:
        load.start()
    for load, store in zip(loads, stores):
        load.wait()
        store.start()
    for store in stores:
        store.wait()


def on_device(
    heads_count,
    hidden,
    parent,
    ssm_state,
    conv_x,
    conv_bc,
    w_gate,
    w_x,
    w_bc,
    w_dt,
    dt_bias,
    a_log,
    d_skip,
    conv_wx,
    conv_wbc,
    norm_gain,
    w_out,
):
    rows_dev, depth = hidden.shape
    _, heads_dev, head_dim, state_dim = ssm_state.shape
    inner = w_x.shape[1]
    bcw = w_bc.shape[1]
    taps = conv_wx.shape[0]
    out_cols = w_out.shape[1] // heads_count
    vmem = pl.BlockSpec(memory_space=pltpu.VMEM)
    hbm = pl.BlockSpec(memory_space=pltpu.HBM)
    dma = pltpu.SemaphoreType.DMA
    sds = jax.ShapeDtypeStruct
    results = pl.pallas_call(
        functools.partial(kernel, heads_count),
        out_shape=(
            sds((rows_dev, out_cols), BF16),
            sds(ssm_state.shape, BF16),
            sds((taps - 1, rows_dev, inner), BF16),
            sds((taps - 1, rows_dev, bcw), BF16),
        ),
        in_specs=[hbm] * 16,
        out_specs=(vmem, hbm, vmem, vmem),
        scratch_shapes=[
            pltpu.VMEM(hidden.shape, BF16),
            pltpu.VMEM((taps - 1, rows_dev, inner), BF16),
            pltpu.VMEM((taps - 1, rows_dev, bcw), BF16),
            pltpu.VMEM((heads_dev, depth), BF16),
            pltpu.VMEM((1, heads_dev), F32),
            pltpu.VMEM((1, heads_dev), F32),
            pltpu.VMEM((1, heads_dev), F32),
            pltpu.VMEM(conv_wx.shape, BF16),
            pltpu.VMEM(conv_wbc.shape, BF16),
            pltpu.VMEM((1, inner), F32),
            pltpu.SMEM(parent.shape, jnp.int32),
            dma((11,)),
            pltpu.VMEM((depth, bcw), BF16),
            pltpu.VMEM((depth, inner), BF16),
            pltpu.VMEM((depth, inner), BF16),
            pltpu.VMEM((heads_count, inner, out_cols), BF16),
            pltpu.VMEM((SPAN * rows_dev, heads_dev, head_dim, state_dim), BF16),
            pltpu.VMEM(ssm_state.shape, BF16),
            pltpu.VMEM((SPAN * rows_dev, taps - 1, inner + bcw), F32),
            pltpu.VMEM((taps - 1, rows_dev, inner + bcw), F32),
            pltpu.VMEM((heads_count, rows_dev, bcw), F32),
            pltpu.VMEM((inner, 2 * rows_dev), F32),
            pltpu.VMEM((heads_count, rows_dev, out_cols + 128), F32),
            pltpu.VMEM((heads_count, rows_dev, out_cols + 128), F32),
            dma,
            dma((CHUNKS,)),
            dma((CHUNKS,)),
            dma((heads_count,)),
            dma,
            dma((rows_dev,)),
            dma((2,)),
            dma((2,)),
            dma((heads_count,)),
            dma((heads_count,)),
            dma((heads_count,)),
            dma((heads_count,)),
        ],
        compiler_params=pltpu.CompilerParams(
            collective_id=0, has_side_effects=True, vmem_limit_bytes=60 * 1024 * 1024
        ),
    )(
        hidden,
        parent,
        ssm_state,
        jnp.transpose(conv_x, (1, 0, 2)),
        jnp.transpose(conv_bc, (1, 0, 2)),
        w_gate,
        w_x,
        w_bc,
        jnp.transpose(w_dt),
        dt_bias.reshape(1, -1),
        a_log.reshape(1, -1),
        d_skip.reshape(1, -1),
        conv_wx,
        conv_wbc,
        norm_gain.reshape(1, -1),
        w_out,
    )
    mixed, new_state, new_cx, new_cbc = pl.pallas_call(
        store_kernel,
        out_shape=tuple(sds(v.shape, v.dtype) for v in results),
        in_specs=[hbm] * 4,
        out_specs=(hbm,) * 4,
        scratch_shapes=[pltpu.VMEM(v.shape, v.dtype) for v in results]
        + [dma((rows_dev + 3,)), dma((rows_dev + 3,))],
        compiler_params=pltpu.CompilerParams(vmem_limit_bytes=60 * 1024 * 1024),
    )(*results)
    return (
        mixed,
        new_state,
        jnp.transpose(new_cx, (1, 0, 2)),
        jnp.transpose(new_cbc, (1, 0, 2)),
    )


def solution(mesh):
    in_specs = (
        P(("groups", "rows"), None),
        P("groups"),
        P(("groups", "rows"), "heads", None, None),
        P(("groups", "rows"), None, "heads"),
        P(("groups", "rows"), None, "heads"),
        P(None, "heads"),
        P(None, "heads"),
        P(None, "heads"),
        P(None, "heads"),
        P("heads"),
        P("heads"),
        P("heads"),
        P(None, "heads"),
        P(None, "heads"),
        P("heads"),
        P("heads", None),
    )
    out_specs = (
        P(("groups", "rows"), "heads"),
        P(("groups", "rows"), "heads", None, None),
        P(("groups", "rows"), None, "heads"),
        P(("groups", "rows"), None, "heads"),
    )
    return jax.shard_map(
        functools.partial(on_device, mesh.shape["heads"]),
        mesh=mesh,
        in_specs=in_specs,
        out_specs=out_specs,
        check_vma=False,
    )
```

```python
import functools

import jax
import jax.numpy as jnp
from jax import lax
from jax.experimental import pallas as pl
from jax.experimental.pallas import tpu as pltpu
from jax.sharding import PartitionSpec as P

SPAN = 2
CHUNKS = 8
MESH = pl.DeviceIdType.MESH
F32 = jnp.float32
BF16 = jnp.bfloat16
NT = (((1,), (1,)), ((), ()))
NN = (((1,), (0,)), ((), ()))


def silu(v):
    return v / (1.0 + jnp.exp(-v))


def kernel(
    heads_count,
    hidden_hbm,
    parent_hbm,
    ssm_state,
    conv_x_hbm,
    conv_bc_hbm,
    w_gate,
    w_x,
    w_bc,
    w_dt_hbm,
    dt_bias_hbm,
    a_log_hbm,
    d_skip_hbm,
    conv_wx_hbm,
    conv_wbc_hbm,
    norm_gain_hbm,
    w_out,
    mixed,
    new_state,
    new_cx,
    new_cbc,
    hidden,
    conv_x,
    conv_bc,
    w_dt,
    dt_bias,
    a_log,
    d_skip,
    conv_wx,
    conv_wbc,
    norm_gain,
    parent,
    in_sem,
    wbc_v,
    wx_v,
    wg_v,
    wo_v,
    st_all,
    ns_v,
    win_all,
    prior_win,
    bc_all,
    cols_t,
    rs_send,
    rs_recv,
    bc_sem,
    x_sem,
    g_sem,
    o_sem,
    st_sem,
    ns_sem,
    pair_send,
    pair_recv,
    bcs_send,
    bcs_recv,
    rss_send,
    rss_recv,
):
    rows_dev, depth = hidden.shape
    heads_dev, head_dim, state_dim = ssm_state.shape[1:]
    inner = w_x.shape[1]
    bcw = w_bc.shape[1]
    out_cols = mixed.shape[1]
    taps = conv_wx.shape[0]
    inner_all = inner * heads_count
    span = depth // CHUNKS

    place = lax.axis_index("rows")
    me = lax.axis_index("heads")
    member = lax.rem(place, SPAN)
    partner = place + 1 - 2 * member
    mine = pl.ds(member * rows_dev, rows_dev)

    def peer(step):
        return lax.rem(me + step, heads_count)

    def chunk_copy(src, dst, sem, k):
        at = pl.ds(pl.multiple_of(k * span, span), span)
        return pltpu.make_async_copy(src.at[at], dst.at[at], sem.at[k])

    def out_copy(step):
        p = peer(step)
        at = pl.ds(pl.multiple_of(p * out_cols, out_cols), out_cols)
        return pltpu.make_async_copy(w_out.at[:, at], wo_v.at[step], o_sem.at[step])

    small = (
        (hidden_hbm, hidden),
        (conv_x_hbm, conv_x),
        (conv_bc_hbm, conv_bc),
        (w_dt_hbm, w_dt),
        (dt_bias_hbm, dt_bias),
        (a_log_hbm, a_log),
        (d_skip_hbm, d_skip),
        (conv_wx_hbm, conv_wx),
        (conv_wbc_hbm, conv_wbc),
        (norm_gain_hbm, norm_gain),
        (parent_hbm, parent),
    )
    loads = [pltpu.make_async_copy(a, b, in_sem.at[i]) for i, (a, b) in enumerate(small)]
    wbc_copy = pltpu.make_async_copy(w_bc, wbc_v, bc_sem)
    for i in (1, 2, 0):
        loads[i].start()
    wbc_copy.start()
    for i in range(3, len(loads)):
        loads[i].start()
    own_state = pltpu.make_async_copy(ssm_state, st_all.at[mine], st_sem)
    out_order = list(range(1, heads_count)) + [0]

    barrier = pltpu.get_barrier_semaphore()
    pl.semaphore_signal(barrier, inc=1, device_id={"rows": partner}, device_id_type=MESH)
    for step in range(1, heads_count):
        pl.semaphore_signal(barrier, inc=1, device_id={"heads": peer(step)}, device_id_type=MESH)

    loads[1].wait()
    loads[2].wait()
    for r in range(rows_dev):
        for k in range(taps - 1):
            win_all[member * rows_dev + r, k : k + 1, :inner] = conv_x[k, r : r + 1, :].astype(F32)
            win_all[member * rows_dev + r, k : k + 1, inner:] = conv_bc[k, r : r + 1, :].astype(F32)

    pl.semaphore_wait(barrier, heads_count)

    win_copy = pltpu.make_async_remote_copy(
        src_ref=win_all.at[mine],
        dst_ref=win_all.at[mine],
        send_sem=pair_send.at[0],
        recv_sem=pair_recv.at[0],
        device_id={"rows": partner},
        device_id_type=MESH,
    )
    win_copy.start()
    state_copy = pltpu.make_async_remote_copy(
        src_ref=ssm_state,
        dst_ref=st_all.at[mine],
        send_sem=pair_send.at[1],
        recv_sem=pair_recv.at[1],
        device_id={"rows": partner},
        device_id_type=MESH,
    )
    for k in range(CHUNKS):
        chunk_copy(w_x, wx_v, x_sem, k).start()
    own_state.start()
    state_copy.start()
    for k in range(CHUNKS):
        chunk_copy(w_gate, wg_v, g_sem, k).start()
    for step in out_order:
        out_copy(step).start()

    loads[0].wait()
    for load in loads[3:]:
        load.wait()
    dt_raw = lax.dot_general(hidden[...], w_dt[...], NT, preferred_element_type=F32)
    wbc_copy.wait()
    bcin = jnp.dot(hidden[...], wbc_v[...], preferred_element_type=F32).astype(BF16).astype(F32)

    win_copy.wait()
    sources = [parent[place * rows_dev + r] for r in range(rows_dev)]
    for r in range(rows_dev):
        for k in range(taps - 1):
            prior_win[k, r : r + 1, :] = win_all[sources[r], k : k + 1, :]

    def window_sum(lo, hi, fresh, taps_ref, out):
        total = fresh * taps_ref[taps - 1 : taps, :].astype(F32)
        for k in range(taps - 1):
            past = prior_win[k, :, lo:hi]
            total += past * taps_ref[k : k + 1, :].astype(F32)
            if k > 0:
                out[k - 1] = past.astype(BF16)
        out[taps - 2] = fresh.astype(BF16)
        return silu(total)

    bconv = window_sum(inner, inner + bcw, bcin, conv_wbc, new_cbc).astype(BF16).astype(F32)
    bc_all[me] = bconv

    def bc_copy(step, slot):
        return pltpu.make_async_remote_copy(
            src_ref=bc_all.at[slot],
            dst_ref=bc_all.at[slot],
            send_sem=bcs_send.at[step],
            recv_sem=bcs_recv.at[slot],
            device_id={"heads": peer(step)},
            device_id_type=MESH,
        )

    for step in range(1, heads_count):
        bc_copy(step, me).start()

    def project(src, dst, sem):
        def step(k, total):
            chunk_copy(src, dst, sem, k).wait()
            at = pl.ds(pl.multiple_of(k * span, span), span)
            return total + jnp.dot(hidden[:, at], dst[at, :], preferred_element_type=F32)

        return lax.fori_loop(0, CHUNKS, step, jnp.zeros((rows_dev, inner), F32))

    xin = project(w_x, wx_v, x_sem).astype(BF16).astype(F32)
    xconv = window_sum(0, inner, xin, conv_wx, new_cx)

    biased = dt_raw + dt_bias[...]
    dt = jnp.maximum(biased, 0.0) + jnp.log1p(jnp.exp(-jnp.abs(biased)))
    decay = jnp.exp(-dt * jnp.exp(a_log[...]))
    head_of = lax.broadcasted_iota(jnp.int32, (heads_dev, inner), 1) // head_dim
    spread = (lax.broadcasted_iota(jnp.int32, (heads_dev, inner), 0) == head_of).astype(F32)

    def per_column(v):
        return lax.dot_general(
            v, spread, NN, precision=lax.Precision.HIGHEST, preferred_element_type=F32
        )

    decay_c = per_column(decay)
    pushed = per_column(dt) * xconv
    skip_c = per_column(d_skip[...])
    cols_t[...] = jnp.transpose(jnp.concatenate([pushed, decay_c], axis=0))

    for step in range(1, heads_count):
        bc_copy(step, peer(step)).wait_recv()

    def maps(first):
        half = heads_count // 2
        parts = [bc_all[first * half + h] for h in range(half)]
        if bcw % 128 == 0:
            return jnp.concatenate(parts, axis=1)
        total = jnp.zeros((rows_dev, state_dim), F32)
        row = lax.broadcasted_iota(jnp.int32, (bcw, state_dim), 0)
        col = lax.broadcasted_iota(jnp.int32, (bcw, state_dim), 1)
        for h in range(half):
            place_h = (row + h * bcw == col).astype(F32)
            total += jnp.dot(parts[h], place_h, preferred_element_type=F32)
        return total

    bmap = maps(0)
    cmap = maps(1)
    cmap_b = cmap.astype(BF16)

    own_state.wait()
    state_copy.wait()
    row_of = lax.broadcasted_iota(jnp.int32, (rows_dev, inner), 0)
    carried = jnp.zeros((rows_dev, inner), F32)
    for r in range(rows_dev):
        block = st_all[sources[r]].reshape(inner, state_dim)
        seen = lax.dot_general(cmap_b, block, NT, preferred_element_type=F32)
        carried = jnp.where(row_of == r, seen, carried)
    overlap = jnp.sum(bmap * cmap, axis=1, keepdims=True)

    def update_rows(first, last):
        for r in range(first, last):
            b_row = bmap[r : r + 1, :]

            def one_head(h, carry, r=r, b_row=b_row):
                at = pl.ds(pl.multiple_of(h * head_dim, head_dim), head_dim)
                cols = cols_t[at, :]
                prior = st_all[sources[r], h].astype(F32)
                value = cols[:, rows_dev + r : rows_dev + r + 1] * prior + cols[:, r : r + 1] * b_row
                ns_v[r, h] = value.astype(BF16)
                return carry

            lax.fori_loop(0, heads_dev, one_head, 0, unroll=2)
            pltpu.make_async_copy(ns_v.at[r], new_state.at[r], ns_sem.at[r]).start()

    early = rows_dev // 2
    update_rows(0, early)
    gate = project(w_gate, wg_v, g_sem)
    y = decay_c * carried + pushed * overlap + skip_c * xconv
    gated = y * silu(gate)
    squares = jnp.sum(gated * gated, axis=1, keepdims=True)
    scaled = (gated * norm_gain[...]).astype(BF16)
    squares_b = jnp.broadcast_to(squares, (rows_dev, 128))

    def rs_copy(step, slot):
        return pltpu.make_async_remote_copy(
            src_ref=rs_send.at[step],
            dst_ref=rs_recv.at[slot],
            send_sem=rss_send.at[step],
            recv_sem=rss_recv.at[slot],
            device_id={"heads": peer(step)},
            device_id_type=MESH,
        )

    for step in out_order:
        out_copy(step).wait()
        terms = jnp.dot(scaled, wo_v[step], preferred_element_type=F32)
        rs_send[step, :, :out_cols] = terms
        rs_send[step, :, out_cols:] = squares_b
        if step > 0:
            rs_copy(step, me).start()

    update_rows(early, rows_dev)

    total = rs_send[0]
    for step in range(1, heads_count):
        rs_copy(step, peer(step)).wait_recv()
        total += rs_recv[peer(step)]
    mean_sq = total[:, out_cols : out_cols + 1] / inner_all
    mixed[...] = (total[:, :out_cols] * lax.rsqrt(mean_sq + 1e-05)).astype(BF16)

    for step in range(1, heads_count):
        bc_copy(step, me).wait_send()
        rs_copy(step, me).wait_send()
    for r in range(rows_dev):
        pltpu.make_async_copy(ns_v.at[r], new_state.at[r], ns_sem.at[r]).wait()


def store_kernel(*refs):
    ins, outs, held = refs[:4], refs[4:8], refs[8:12]
    in_sem, out_sem = refs[12:]
    rows_dev = ins[1].shape[0]
    loads = [pltpu.make_async_copy(ins[1].at[r], held[1].at[r], in_sem.at[r]) for r in range(rows_dev)]
    stores = [pltpu.make_async_copy(held[1].at[r], outs[1].at[r], out_sem.at[r]) for r in range(rows_dev)]
    for n, i in enumerate((0, 2, 3)):
        loads.append(pltpu.make_async_copy(ins[i], held[i], in_sem.at[rows_dev + n]))
        stores.append(pltpu.make_async_copy(held[i], outs[i], out_sem.at[rows_dev + n]))
    for load in loads:
        load.start()
    for load, store in zip(loads, stores):
        load.wait()
        store.start()
    for store in stores:
        store.wait()


def on_device(
    heads_count,
    hidden,
    parent,
    ssm_state,
    conv_x,
    conv_bc,
    w_gate,
    w_x,
    w_bc,
    w_dt,
    dt_bias,
    a_log,
    d_skip,
    conv_wx,
    conv_wbc,
    norm_gain,
    w_out,
):
    rows_dev, depth = hidden.shape
    _, heads_dev, head_dim, state_dim = ssm_state.shape
    inner = w_x.shape[1]
    bcw = w_bc.shape[1]
    taps = conv_wx.shape[0]
    out_cols = w_out.shape[1] // heads_count
    vmem = pl.BlockSpec(memory_space=pltpu.VMEM)
    hbm = pl.BlockSpec(memory_space=pltpu.HBM)
    dma = pltpu.SemaphoreType.DMA
    sds = jax.ShapeDtypeStruct
    results = pl.pallas_call(
        functools.partial(kernel, heads_count),
        out_shape=(
            sds((rows_dev, out_cols), BF16),
            sds(ssm_state.shape, BF16),
            sds((taps - 1, rows_dev, inner), BF16),
            sds((taps - 1, rows_dev, bcw), BF16),
        ),
        in_specs=[hbm] * 16,
        out_specs=(vmem, hbm, vmem, vmem),
        scratch_shapes=[
            pltpu.VMEM(hidden.shape, BF16),
            pltpu.VMEM((taps - 1, rows_dev, inner), BF16),
            pltpu.VMEM((taps - 1, rows_dev, bcw), BF16),
            pltpu.VMEM((heads_dev, depth), BF16),
            pltpu.VMEM((1, heads_dev), F32),
            pltpu.VMEM((1, heads_dev), F32),
            pltpu.VMEM((1, heads_dev), F32),
            pltpu.VMEM(conv_wx.shape, BF16),
            pltpu.VMEM(conv_wbc.shape, BF16),
            pltpu.VMEM((1, inner), F32),
            pltpu.SMEM(parent.shape, jnp.int32),
            dma((11,)),
            pltpu.VMEM((depth, bcw), BF16),
            pltpu.VMEM((depth, inner), BF16),
            pltpu.VMEM((depth, inner), BF16),
            pltpu.VMEM((heads_count, inner, out_cols), BF16),
            pltpu.VMEM((SPAN * rows_dev, heads_dev, head_dim, state_dim), BF16),
            pltpu.VMEM(ssm_state.shape, BF16),
            pltpu.VMEM((SPAN * rows_dev, taps - 1, inner + bcw), F32),
            pltpu.VMEM((taps - 1, rows_dev, inner + bcw), F32),
            pltpu.VMEM((heads_count, rows_dev, bcw), F32),
            pltpu.VMEM((inner, 2 * rows_dev), F32),
            pltpu.VMEM((heads_count, rows_dev, out_cols + 128), F32),
            pltpu.VMEM((heads_count, rows_dev, out_cols + 128), F32),
            dma,
            dma((CHUNKS,)),
            dma((CHUNKS,)),
            dma((heads_count,)),
            dma,
            dma((rows_dev,)),
            dma((2,)),
            dma((2,)),
            dma((heads_count,)),
            dma((heads_count,)),
            dma((heads_count,)),
            dma((heads_count,)),
        ],
        compiler_params=pltpu.CompilerParams(
            collective_id=0, has_side_effects=True, vmem_limit_bytes=60 * 1024 * 1024
        ),
    )(
        hidden,
        parent,
        ssm_state,
        jnp.transpose(conv_x, (1, 0, 2)),
        jnp.transpose(conv_bc, (1, 0, 2)),
        w_gate,
        w_x,
        w_bc,
        jnp.transpose(w_dt),
        dt_bias.reshape(1, -1),
        a_log.reshape(1, -1),
        d_skip.reshape(1, -1),
        conv_wx,
        conv_wbc,
        norm_gain.reshape(1, -1),
        w_out,
    )
    mixed, new_state, new_cx, new_cbc = pl.pallas_call(
        store_kernel,
        out_shape=tuple(sds(v.shape, v.dtype) for v in results),
        in_specs=[hbm] * 4,
        out_specs=(hbm,) * 4,
        scratch_shapes=[pltpu.VMEM(v.shape, v.dtype) for v in results]
        + [dma((rows_dev + 3,)), dma((rows_dev + 3,))],
        compiler_params=pltpu.CompilerParams(vmem_limit_bytes=60 * 1024 * 1024),
    )(*results)
    return (
        mixed,
        new_state,
        jnp.transpose(new_cx, (1, 0, 2)),
        jnp.transpose(new_cbc, (1, 0, 2)),
    )


def solution(mesh):
    in_specs = (
        P(("groups", "rows"), None),
        P("groups"),
        P(("groups", "rows"), "heads", None, None),
        P(("groups", "rows"), None, "heads"),
        P(("groups", "rows"), None, "heads"),
        P(None, "heads"),
        P(None, "heads"),
        P(None, "heads"),
        P(None, "heads"),
        P("heads"),
        P("heads"),
        P("heads"),
        P(None, "heads"),
        P(None, "heads"),
        P("heads"),
        P("heads", None),
    )
    out_specs = (
        P(("groups", "rows"), "heads"),
        P(("groups", "rows"), "heads", None, None),
        P(("groups", "rows"), None, "heads"),
        P(("groups", "rows"), None, "heads"),
    )
    return jax.shard_map(
        functools.partial(on_device, mesh.shape["heads"]),
        mesh=mesh,
        in_specs=in_specs,
        out_specs=out_specs,
        check_vma=False,
    )
```
